32 devices in a mesh: blk: 4 (over z), pen: 8 (over y, x, core).
Axes of the slice: x: 2, y: 2, z: 4, core: 2. Of those that a mesh axis runs over, the one named last changes fastest.
Arguments:
- state: bfloat16 [4, 2, 32, 512, 512], P('blk', None, None, 'pen'), may hold values from -6 to 6
- inverse_x: bfloat16 [4, 2, 512, 512], P('blk')
- inverse_y: bfloat16 [4, 2, 512, 512], P('blk')
- rates: float32 [4, 3], P('blk'), may hold values from 0.05 to 0.4
- partner: int32 [4, 2], P('blk'), may hold values from 0 to 3
- face_side: int32 [4, 2], P('blk'), may hold values from 0 to 1
- orient: int32 [4, 2], P('blk'), may hold values from 0 to 1
- offset: int32 [4, 2], P('blk'), may hold values from 0 to 7
Outputs:
- relaxed: bfloat16 [4, 2, 32, 512, 512], P('blk', None, None, 'pen')
The draws below stay inside these ranges and needn't reach their ends.
All inputs are finite; a program needn't handle non-finite values.
Results may differ from the reference program's by a relative error of at most 0.0058.
Values may be sent and summed in bfloat16 or wider, within the bound.
A program may use at most 64 MiB of HBM per device.

```python
import math
import jax
import jax.numpy as jnp
from jax import lax

GX = 512
GY = 512
GZ = 32
STEPS = 2
NB = 4
ROWS = 64
N_PEN = 8


def draw_inverse_x(key, part):
    k_diag, k_off = jax.random.split(jax.random.fold_in(key, 11))
    diagonal = jax.random.uniform(k_diag, (NB, 2, GX), jnp.float32, 0.6, 1.2)
    spread_off = jax.random.normal(k_off, (NB, 2, GX, GX), jnp.float32) * (0.5 / math.sqrt(GX))
    identity = jnp.eye(GX, dtype=jnp.float32)
    return (spread_off * (1.0 - identity) + diagonal[..., None] * identity).astype(jnp.bfloat16)


def draw_inverse_y(key, part):
    k_diag, k_off = jax.random.split(jax.random.fold_in(key, 23))
    diagonal = jax.random.uniform(k_diag, (NB, 2, GY), jnp.float32, 0.6, 1.2)
    spread_off = jax.random.normal(k_off, (NB, 2, GY, GY), jnp.float32) * (0.5 / math.sqrt(GY))
    identity = jnp.eye(GY, dtype=jnp.float32)
    return (spread_off * (1.0 - identity) + diagonal[..., None] * identity).astype(jnp.bfloat16)


def plant(array, stream_key, least, largest):
    place = [jax.random.randint(jax.random.fold_in(stream_key, axis), (), 0, length) for axis, length in enumerate(array.shape)]
    longest = array.shape.index(max(array.shape))
    neighbour = place[:longest] + [(place[longest] + 1) % array.shape[longest]] + place[longest + 1:]
    return array.at[tuple(place)].set(least).at[tuple(neighbour)].set(largest)


def block_scale(rng, dims, cuts, least, high):
    def one(axis_at, shards_of):
        heights = jax.random.uniform(jax.random.fold_in(jax.random.fold_in(rng, 6), axis_at), (shards_of,), jnp.float32, least / len(cuts), high / len(cuts))
        return jnp.repeat(jnp.exp(heights), dims[axis_at] // shards_of).reshape((-1,) + (1,) * (len(dims) - axis_at - 1))

    factor_of = one(*cuts[0])
    for cut in cuts[1:]:
        factor_of = factor_of * one(*cut)
    return factor_of


def noise(key, dims, spread, limit, shards=(), held_as=jnp.bfloat16):
    array = jax.random.normal(key, dims, jnp.float32) * spread
    if len(shards) > 0:
        array = block_scale(key, dims, shards, -0.22, 0.18) * array
    return jnp.clip(array, min=-limit, max=limit).astype(held_as)


def setup_inputs(seed: int = 0) -> dict:
    splits = jax.random.split(jax.random.key(seed), 9)
    return {
        "state": noise(splits[0], (NB, 2, GZ, GY, GX), 1.0, 6.0, ((0, 4), (3, 8))),
        "inverse_x": draw_inverse_x(jax.random.fold_in(splits[8], 71), 0),
        "inverse_y": draw_inverse_y(jax.random.fold_in(splits[8], 71), 0),
        "rates": jnp.clip(jnp.exp(math.log(0.4) - 2.0794415 * jax.random.uniform(splits[3], (NB, 3), jnp.float32) ** block_scale(splits[3], (NB, 3), ((0, 4),), -0.2, 0.2)), 0.05, 0.4),
        "partner": plant(jax.random.randint(splits[4], (NB, 2), 0, NB), jax.random.fold_in(splits[4], 1), 0, NB - 1).astype(jnp.int32),
        "face_side": plant(jax.random.randint(splits[5], (NB, 2), 0, 2), jax.random.fold_in(splits[5], 1), 0, 1).astype(jnp.int32),
        "orient": plant(jax.random.randint(splits[6], (NB, 2), 0, 2), jax.random.fold_in(splits[6], 1), 0, 1).astype(jnp.int32),
        "offset": plant(jax.random.randint(splits[7], (NB, 2), 0, N_PEN), jax.random.fold_in(splits[7], 1), 0, N_PEN - 1).astype(jnp.int32),
    }


def reference(state, inverse_x, inverse_y, rates, partner, face_side, orient, offset):
    rows_y = jnp.arange(GY, dtype=jnp.int32)
    magnet = state
    for repeat in range(STEPS):
        layers = jnp.stack([magnet[..., 0], magnet[..., GX - 1]], axis=1)

        def advance(inputs):
            block_cells, inv_x, inv_y, rate_row, partner_row, side_row, orient_row, offset_row = inputs
            ghosts = []
            for which in range(2):
                source = layers[partner_row[which], side_row[which]]
                mirrored = jnp.where(orient_row[which] == 1, GY - 1 - rows_y, rows_y)
                take_at = ((mirrored + offset_row[which] * ROWS) % GY).astype(jnp.int32)
                ghosts.append(jnp.take(source, take_at, axis=-1).astype(jnp.float32))
            interior = jnp.einsum('fax,fzyx->fzya', inv_x.astype(jnp.float32), block_cells.astype(jnp.float32))
            first_col = inv_x[:, :, 0].astype(jnp.float32)
            last_col = inv_x[:, :, GX - 1].astype(jnp.float32)
            swept_x = interior + first_col[:, None, None, :] * ghosts[0][..., None] + last_col[:, None, None, :] * ghosts[1][..., None]
            swept_x = lax.optimization_barrier(swept_x.astype(jnp.bfloat16))
            swept_y = jnp.einsum('fcy,fzyx->fzcx', inv_y.astype(jnp.float32), swept_x.astype(jnp.float32))
            proton = swept_y[0]
            carbon = swept_y[1]
            new_proton = proton - (rate_row[0] * proton + rate_row[2] * carbon)
            new_carbon = carbon - (rate_row[1] * carbon + rate_row[2] * proton)
            return jnp.stack([new_proton, new_carbon]).astype(jnp.bfloat16)

        magnet = lax.map(advance, (magnet, inverse_x, inverse_y, rates, partner, face_side, orient, offset))
    return magnet
```

```python
import functools
import jax
import jax.numpy as jnp
from jax import lax
from jax.experimental import pallas as pl
from jax.experimental.pallas import tpu as pltpu
from jax.sharding import PartitionSpec as P

STEPS = 2
LANES = 128
NT = (((1,), (1,)), ((), ()))


def dot(a, b):
    return jnp.dot(a, b, preferred_element_type=jnp.float32)


def dot_nt(a, b):
    return lax.dot_general(a, b, NT, preferred_element_type=jnp.float32)


def kernel(n_pen, n_blk, rates, partner, side, orient, offset, state, inv_x, inv_y, out,
           planes, swept, op_x, op_xt, op_y, perm, layers,
           in_send, in_recv, out_send, out_recv, g_send, g_recv, own_sem, op_sem):
    blk = lax.axis_index("blk")
    pen = lax.axis_index("pen")
    rows = state.shape[3]
    z_per = planes.shape[1]
    gy, gx = planes.shape[2], planes.shape[3]

    barrier = pltpu.get_barrier_semaphore()
    for d in range(1, n_pen):
        pl.semaphore_signal(barrier, inc=1, device_id=(blk, lax.rem(pen + d, n_pen)),
                            device_id_type=pl.DeviceIdType.MESH)
    for d in range(1, n_blk):
        pl.semaphore_signal(barrier, inc=1, device_id=(lax.rem(blk + d, n_blk), pen),
                            device_id_type=pl.DeviceIdType.MESH)
    pl.semaphore_wait(barrier, n_pen + n_blk - 2)

    def in_copy(z, d):
        to = lax.rem(pen + d, n_pen)
        return pltpu.make_async_remote_copy(
            src_ref=state.at[0, :, to * z_per + z],
            dst_ref=planes.at[:, z, pl.ds(pen * rows, rows)],
            send_sem=in_send.at[z, d], recv_sem=in_recv.at[z, d],
            device_id=(blk, to), device_id_type=pl.DeviceIdType.MESH)

    def in_arrival(z, d):
        came = lax.rem(pen + n_pen - d, n_pen)
        return pltpu.make_async_remote_copy(
            src_ref=state.at[0, :, came * z_per + z],
            dst_ref=planes.at[:, z, pl.ds(came * rows, rows)],
            send_sem=in_send.at[z, d], recv_sem=in_recv.at[z, d],
            device_id=(blk, came), device_id_type=pl.DeviceIdType.MESH)

    def in_own(z):
        return pltpu.make_async_copy(
            state.at[0, :, pen * z_per + z], planes.at[:, z, pl.ds(pen * rows, rows)], own_sem.at[0, z])

    def out_copy(z, d):
        to = lax.rem(pen + d, n_pen)
        return pltpu.make_async_remote_copy(
            src_ref=planes.at[:, z, pl.ds(to * rows, rows)],
            dst_ref=out.at[0, :, pen * z_per + z],
            send_sem=out_send.at[z, d], recv_sem=out_recv.at[z, d],
            device_id=(blk, to), device_id_type=pl.DeviceIdType.MESH)

    def out_arrival(z, d):
        came = lax.rem(pen + n_pen - d, n_pen)
        return pltpu.make_async_remote_copy(
            src_ref=planes.at[:, z, pl.ds(came * rows, rows)],
            dst_ref=out.at[0, :, came * z_per + z],
            send_sem=out_send.at[z, d], recv_sem=out_recv.at[z, d],
            device_id=(blk, came), device_id_type=pl.DeviceIdType.MESH)

    def out_own(z):
        return pltpu.make_async_copy(
            planes.at[:, z, pl.ds(pen * rows, rows)], out.at[0, :, pen * z_per + z], own_sem.at[1, z])

    def ghost_copy(slot, d):
        return pltpu.make_async_remote_copy(
            src_ref=layers.at[slot, blk], dst_ref=layers.at[slot, blk],
            send_sem=g_send.at[slot, d], recv_sem=g_recv.at[slot, d],
            device_id=(lax.rem(blk + d, n_blk), pen), device_id_type=pl.DeviceIdType.MESH)

    def ghost_arrival(slot, d):
        came = lax.rem(blk + n_blk - d, n_blk)
        return pltpu.make_async_remote_copy(
            src_ref=layers.at[slot, came], dst_ref=layers.at[slot, came],
            send_sem=g_send.at[slot, d], recv_sem=g_recv.at[slot, d],
            device_id=(came, pen), device_id_type=pl.DeviceIdType.MESH)

    @pl.loop(0, z_per)
    def _(z):
        for d in range(1, n_pen):
            in_copy(z, d).start()
        in_own(z).start()

    load_x = pltpu.make_async_copy(inv_x.at[0], op_x, op_sem.at[0])
    load_y = pltpu.make_async_copy(inv_y.at[0], op_y, op_sem.at[1])
    load_x.start()
    load_y.start()

    at_j = lax.broadcasted_iota(jnp.int32, (gy, gy), 0)
    at_y = lax.broadcasted_iota(jnp.int32, (gy, gy), 1)
    for k in range(2):
        take = jnp.where(orient[0, k] == 1, gy - 1 - at_j, at_j) + offset[0, k] * rows
        take = jnp.where(take >= gy, take - gy, take)
        perm[k] = jnp.where(take == at_y, 1.0, 0.0).astype(jnp.bfloat16)
    eye = jnp.where(at_j == at_y, 1.0, 0.0).astype(jnp.bfloat16)
    load_x.wait()
    for f in range(2):
        op_xt[f] = dot_nt(eye, op_x[f]).astype(jnp.bfloat16)
    load_y.wait()

    pick_row = lax.broadcasted_iota(jnp.int32, (16, LANES), 0)
    pick_lane = lax.broadcasted_iota(jnp.int32, (16, LANES), 1)
    lane = lax.broadcasted_iota(jnp.int32, (gy, LANES), 1)
    ends = ((0, 0), (gx - LANES, LANES - 1))
    half = gx // 2

    @pl.loop(0, z_per)
    def _(z):
        for d in range(1, n_pen):
            in_arrival(z, d).wait_recv()
        in_own(z).wait()

        @pl.loop(0, STEPS)
        def _(step):
            slot = z * STEPS + step
            mine = jnp.zeros((16, gy), jnp.float32)
            for k, (first, at) in enumerate(ends):
                for f in range(2):
                    pick = jnp.where((pick_row == 2 * k + f) & (pick_lane == at), 1.0, 0.0).astype(jnp.bfloat16)
                    mine += dot_nt(pick, planes[f, z, :, first:first + LANES])
            layers[slot, blk] = mine.astype(jnp.bfloat16)
            for d in range(1, n_blk):
                ghost_copy(slot, d).start()
            for d in range(1, n_blk):
                ghost_arrival(slot, d).wait_recv()

            for k, (first, at) in enumerate(ends):
                layer = layers[slot, 0]
                for b in range(1, n_blk):
                    layer = jnp.where(partner[0, k] == b, layers[slot, b], layer)
                ghosts = dot_nt(perm[k], layer)
                for f in range(2):
                    ghost = jnp.where(side[0, k] == 1, ghosts[:, 2 + f:3 + f], ghosts[:, f:f + 1])
                    cells = planes[f, z, :, first:first + LANES].astype(jnp.float32)
                    planes[f, z, :, first:first + LANES] = (
                        cells + jnp.where(lane == at, ghost, 0.0)).astype(jnp.bfloat16)

            for f in range(2):
                for n in range(2):
                    swept[f, :, n * half:(n + 1) * half] = dot(
                        planes[f, z], op_xt[f, :, n * half:(n + 1) * half]).astype(jnp.bfloat16)
            for n in range(2):
                proton = dot(op_y[0], swept[0, :, n * half:(n + 1) * half])
                carbon = dot(op_y[1], swept[1, :, n * half:(n + 1) * half])
                new_proton = proton - (rates[0, 0] * proton + rates[0, 2] * carbon)
                new_carbon = carbon - (rates[0, 1] * carbon + rates[0, 2] * proton)
                planes[0, z, :, n * half:(n + 1) * half] = new_proton.astype(jnp.bfloat16)
                planes[1, z, :, n * half:(n + 1) * half] = new_carbon.astype(jnp.bfloat16)

        for d in range(1, n_pen):
            out_copy(z, d).start()
        out_own(z).start()

    @pl.loop(0, z_per)
    def _(z):
        for d in range(1, n_pen):
            in_copy(z, d).wait_send()
            out_copy(z, d).wait_send()
            out_arrival(z, d).wait_recv()
        out_own(z).wait()
        for step in range(STEPS):
            for d in range(1, n_blk):
                ghost_copy(z * STEPS + step, d).wait_send()


def solution(mesh):
    n_pen, n_blk = mesh.shape["pen"], mesh.shape["blk"]

    def local(state, inverse_x, inverse_y, rates, partner, face_side, orient, offset):
        _, fields, gz, rows, gx = state.shape
        z_per, gy = gz // n_pen, rows * n_pen
        slots = z_per * STEPS
        smem = pl.BlockSpec(memory_space=pltpu.SMEM)
        anywhere = pl.BlockSpec(memory_space=pl.ANY)
        bf16 = jnp.bfloat16
        return pl.pallas_call(
            functools.partial(kernel, n_pen, n_blk),
            out_shape=jax.ShapeDtypeStruct(state.shape, state.dtype),
            in_specs=[smem] * 5 + [anywhere] * 3,
            out_specs=anywhere,
            scratch_shapes=[
                pltpu.VMEM((fields, z_per, gy, gx), bf16),
                pltpu.VMEM((fields, gy, gx), bf16),
                pltpu.VMEM((fields, gx, gx), bf16),
                pltpu.VMEM((fields, gx, gx), bf16),
                pltpu.VMEM((fields, gy, gy), bf16),
                pltpu.VMEM((2, gy, gy), bf16),
                pltpu.VMEM((slots, n_blk, 16, gy), bf16),
                pltpu.SemaphoreType.DMA((z_per, n_pen)),
                pltpu.SemaphoreType.DMA((z_per, n_pen)),
                pltpu.SemaphoreType.DMA((z_per, n_pen)),
                pltpu.SemaphoreType.DMA((z_per, n_pen)),
                pltpu.SemaphoreType.DMA((slots, n_blk)),
                pltpu.SemaphoreType.DMA((slots, n_blk)),
                pltpu.SemaphoreType.DMA((2, z_per)),
                pltpu.SemaphoreType.DMA((2,)),
            ],
            compiler_params=pltpu.CompilerParams(
                collective_id=0, has_side_effects=True, vmem_limit_bytes=60 * 1024 * 1024),
            cost_estimate=pl.CostEstimate(
                flops=8 * STEPS * z_per * gy * gx * (gx + gy) // 2,
                bytes_accessed=4 * state.size + 8 * gx * gx, transcendentals=0),
        )(rates, partner, face_side, orient, offset, state, inverse_x, inverse_y)

    line = P("blk", None)
    return jax.shard_map(
        local,
        mesh=mesh,
        in_specs=(
            P("blk", None, None, "pen", None),
            P("blk", None, None, None),
            P("blk", None, None, None),
            line, line, line, line, line,
        ),
        out_specs=P("blk", None, None, "pen", None),
        check_vma=False,
    )
```

```python
import functools
import jax
import jax.numpy as jnp
from jax import lax
from jax.experimental import pallas as pl
from jax.experimental.pallas import tpu as pltpu
from jax.sharding import PartitionSpec as P

STEPS = 2
LANES = 128
NT = (((1,), (1,)), ((), ()))


def dot(a, b):
    return jnp.dot(a, b, preferred_element_type=jnp.float32)


def dot_nt(a, b):
    return lax.dot_general(a, b, NT, preferred_element_type=jnp.float32)


def partner_of(pen, d, n_pen):
    if n_pen & (n_pen - 1) or n_pen < 8:
        return lax.rem(pen + d, n_pen)
    core = lax.rem(pen, 2)
    swapped = (d & ~6) | (d & 2) << 1 | (d & 4) >> 1
    other = pen
    for bit in (1 << b for b in range(n_pen.bit_length() - 1)):
        flip = (1 - core) * int(d & bit > 0) + core * int(swapped & bit > 0)
        other = other + flip * bit * (1 - 2 * lax.rem(pen // bit, 2))
    return other


def kernel(n_pen, n_blk, rates, partner, side, orient, offset, state, inv_x, inv_y, out,
           planes, swept, op_x, op_xt, op_y, perm, layers,
           in_send, in_recv, out_send, out_recv, g_send, g_recv, own_sem, op_sem):
    blk = lax.axis_index("blk")
    pen = lax.axis_index("pen")
    rows = state.shape[3]
    z_per = planes.shape[1]
    gy, gx = planes.shape[2], planes.shape[3]

    order = (2, 4, 6, 3, 5, 7, 1) if n_pen == 8 else range(1, n_pen)
    partners = [partner_of(pen, d, n_pen) for d in order]

    barrier = pltpu.get_barrier_semaphore()
    for to in partners:
        pl.semaphore_signal(barrier, inc=1, device_id=(blk, to),
                            device_id_type=pl.DeviceIdType.MESH)
    for d in range(1, n_blk):
        pl.semaphore_signal(barrier, inc=1, device_id=(lax.rem(blk + d, n_blk), pen),
                            device_id_type=pl.DeviceIdType.MESH)
    pl.semaphore_wait(barrier, n_pen + n_blk - 2)

    def in_copy(z, to):
        return pltpu.make_async_remote_copy(
            src_ref=state.at[0, :, to * z_per + z],
            dst_ref=planes.at[:, z, pl.ds(pen * rows, rows)],
            send_sem=in_send.at[z, to], recv_sem=in_recv.at[z, pen],
            device_id=(blk, to), device_id_type=pl.DeviceIdType.MESH)

    def in_arrival(z, came):
        return pltpu.make_async_remote_copy(
            src_ref=state.at[0, :, came * z_per + z],
            dst_ref=planes.at[:, z, pl.ds(came * rows, rows)],
            send_sem=in_send.at[z, came], recv_sem=in_recv.at[z, came],
            device_id=(blk, came), device_id_type=pl.DeviceIdType.MESH)

    def in_own(z):
        return pltpu.make_async_copy(
            state.at[0, :, pen * z_per + z], planes.at[:, z, pl.ds(pen * rows, rows)], own_sem.at[0, z])

    def out_copy(z, to):
        return pltpu.make_async_remote_copy(
            src_ref=planes.at[:, z, pl.ds(to * rows, rows)],
            dst_ref=out.at[0, :, pen * z_per + z],
            send_sem=out_send.at[z, to], recv_sem=out_recv.at[z, pen],
            device_id=(blk, to), device_id_type=pl.DeviceIdType.MESH)

    def out_arrival(z, came):
        return pltpu.make_async_remote_copy(
            src_ref=planes.at[:, z, pl.ds(came * rows, rows)],
            dst_ref=out.at[0, :, came * z_per + z],
            send_sem=out_send.at[z, came], recv_sem=out_recv.at[z, came],
            device_id=(blk, came), device_id_type=pl.DeviceIdType.MESH)

    def out_own(z):
        return pltpu.make_async_copy(
            planes.at[:, z, pl.ds(pen * rows, rows)], out.at[0, :, pen * z_per + z], own_sem.at[1, z])

    def ghost_copy(slot, d):
        return pltpu.make_async_remote_copy(
            src_ref=layers.at[slot, blk], dst_ref=layers.at[slot, blk],
            send_sem=g_send.at[slot, d], recv_sem=g_recv.at[slot, d],
            device_id=(lax.rem(blk + d, n_blk), pen), device_id_type=pl.DeviceIdType.MESH)

    def ghost_arrival(slot, d):
        came = lax.rem(blk + n_blk - d, n_blk)
        return pltpu.make_async_remote_copy(
            src_ref=layers.at[slot, came], dst_ref=layers.at[slot, came],
            send_sem=g_send.at[slot, d], recv_sem=g_recv.at[slot, d],
            device_id=(came, pen), device_id_type=pl.DeviceIdType.MESH)

    def send_in(z):
        for to in partners:
            in_copy(z, to).start()
        in_own(z).start()

    ahead = min(2, z_per)
    pl.loop(0, ahead)(send_in)

    load_x = pltpu.make_async_copy(inv_x.at[0], op_x, op_sem.at[0])
    load_y = pltpu.make_async_copy(inv_y.at[0], op_y, op_sem.at[1])
    load_x.start()
    load_y.start()

    at_j = lax.broadcasted_iota(jnp.int32, (gy, gy), 0)
    at_y = lax.broadcasted_iota(jnp.int32, (gy, gy), 1)
    for k in range(2):
        take = jnp.where(orient[0, k] == 1, gy - 1 - at_j, at_j) + offset[0, k] * rows
        take = jnp.where(take >= gy, take - gy, take)
        perm[k] = jnp.where(take == at_y, 1.0, 0.0).astype(jnp.bfloat16)
    eye = jnp.where(at_j == at_y, 1.0, 0.0).astype(jnp.bfloat16)
    load_x.wait()
    for f in range(2):
        op_xt[f] = dot_nt(eye, op_x[f]).astype(jnp.bfloat16)
    load_y.wait()

    pick_row = lax.broadcasted_iota(jnp.int32, (16, LANES), 0)
    pick_lane = lax.broadcasted_iota(jnp.int32, (16, LANES), 1)
    lane = lax.broadcasted_iota(jnp.int32, (gy, LANES), 1)
    ends = ((0, 0), (gx - LANES, LANES - 1))
    half = gx // 2

    @pl.loop(0, z_per)
    def _(z):
        for came in partners:
            in_arrival(z, came).wait_recv()
        in_own(z).wait()
        pl.when(z + ahead < z_per)(lambda: send_in(z + ahead))

        @pl.loop(0, STEPS)
        def _(step):
            slot = z * STEPS + step
            mine = jnp.zeros((16, gy), jnp.float32)
            for k, (first, at) in enumerate(ends):
                for f in range(2):
                    pick = jnp.where((pick_row == 2 * k + f) & (pick_lane == at), 1.0, 0.0).astype(jnp.bfloat16)
                    mine += dot_nt(pick, planes[f, z, :, first:first + LANES])
            layers[slot, blk] = mine.astype(jnp.bfloat16)
            for d in range(1, n_blk):
                ghost_copy(slot, d).start()
            for d in range(1, n_blk):
                ghost_arrival(slot, d).wait_recv()

            for k, (first, at) in enumerate(ends):
                layer = layers[slot, 0]
                for b in range(1, n_blk):
                    layer = jnp.where(partner[0, k] == b, layers[slot, b], layer)
                ghosts = dot_nt(perm[k], layer)
                for f in range(2):
                    ghost = jnp.where(side[0, k] == 1, ghosts[:, 2 + f:3 + f], ghosts[:, f:f + 1])
                    cells = planes[f, z, :, first:first + LANES].astype(jnp.float32)
                    planes[f, z, :, first:first + LANES] = (
                        cells + jnp.where(lane == at, ghost, 0.0)).astype(jnp.bfloat16)

            for f in range(2):
                for n in range(2):
                    swept[f, :, n * half:(n + 1) * half] = dot(
                        planes[f, z], op_xt[f, :, n * half:(n + 1) * half]).astype(jnp.bfloat16)
            for n in range(2):
                proton = dot(op_y[0], swept[0, :, n * half:(n + 1) * half])
                carbon = dot(op_y[1], swept[1, :, n * half:(n + 1) * half])
                new_proton = proton - (rates[0, 0] * proton + rates[0, 2] * carbon)
                new_carbon = carbon - (rates[0, 1] * carbon + rates[0, 2] * proton)
                planes[0, z, :, n * half:(n + 1) * half] = new_proton.astype(jnp.bfloat16)
                planes[1, z, :, n * half:(n + 1) * half] = new_carbon.astype(jnp.bfloat16)

        for to in partners:
            out_copy(z, to).start()
        out_own(z).start()

    @pl.loop(0, z_per)
    def _(z):
        for to in partners:
            in_copy(z, to).wait_send()
            out_copy(z, to).wait_send()
            out_arrival(z, to).wait_recv()
        out_own(z).wait()
        for step in range(STEPS):
            for d in range(1, n_blk):
                ghost_copy(z * STEPS + step, d).wait_send()


def solution(mesh):
    n_pen, n_blk = mesh.shape["pen"], mesh.shape["blk"]

    def local(state, inverse_x, inverse_y, rates, partner, face_side, orient, offset):
        _, fields, gz, rows, gx = state.shape
        z_per, gy = gz // n_pen, rows * n_pen
        slots = z_per * STEPS
        keep = functools.partial(pltpu.with_memory_space_constraint, memory_space=pltpu.HBM)
        smem = pl.BlockSpec(memory_space=pltpu.SMEM)
        anywhere = pl.BlockSpec(memory_space=pl.ANY)
        bf16 = jnp.bfloat16
        return pl.pallas_call(
            functools.partial(kernel, n_pen, n_blk),
            out_shape=pltpu.VMEM(state.shape, state.dtype),
            in_specs=[smem] * 5 + [anywhere] * 3,
            out_specs=anywhere,
            scratch_shapes=[
                pltpu.VMEM((fields, z_per, gy, gx), bf16),
                pltpu.VMEM((fields, gy, gx), bf16),
                pltpu.VMEM((fields, gx, gx), bf16),
                pltpu.VMEM((fields, gx, gx), bf16),
                pltpu.VMEM((fields, gy, gy), bf16),
                pltpu.VMEM((2, gy, gy), bf16),
                pltpu.VMEM((slots, n_blk, 16, gy), bf16),
                pltpu.SemaphoreType.DMA((z_per, n_pen)),
                pltpu.SemaphoreType.DMA((z_per, n_pen)),
                pltpu.SemaphoreType.DMA((z_per, n_pen)),
                pltpu.SemaphoreType.DMA((z_per, n_pen)),
                pltpu.SemaphoreType.DMA((slots, n_blk)),
                pltpu.SemaphoreType.DMA((slots, n_blk)),
                pltpu.SemaphoreType.DMA((2, z_per)),
                pltpu.SemaphoreType.DMA((2,)),
            ],
            compiler_params=pltpu.CompilerParams(
                collective_id=0, has_side_effects=True, vmem_limit_bytes=48 * 1024 * 1024),
            cost_estimate=pl.CostEstimate(
                flops=8 * STEPS * z_per * gy * gx * (gx + gy) // 2,
                bytes_accessed=4 * state.size + 8 * gx * gx, transcendentals=0),
        )(*map(keep, (rates, partner, face_side, orient, offset, state, inverse_x, inverse_y)))

    line = P("blk", None)
    return jax.shard_map(
        local,
        mesh=mesh,
        in_specs=(
            P("blk", None, None, "pen", None),
            P("blk", None, None, None),
            P("blk", None, None, None),
            line, line, line, line, line,
        ),
        out_specs=P("blk", None, None, "pen", None),
        check_vma=False,
    )
```

```python
import functools
import jax
import jax.numpy as jnp
from jax import lax
from jax.experimental import pallas as pl
from jax.experimental.pallas import tpu as pltpu
from jax.sharding import PartitionSpec as P

STEPS = 2
LANES = 128
NT = (((1,), (1,)), ((), ()))


def dot(a, b):
    return jnp.dot(a, b, preferred_element_type=jnp.float32)


def dot_nt(a, b):
    return lax.dot_general(a, b, NT, preferred_element_type=jnp.float32)


def partner_of(pen, d, n_pen):
    if n_pen & (n_pen - 1) or n_pen < 8:
        return lax.rem(pen + d, n_pen)
    core = lax.rem(pen, 2)
    swapped = (d & ~6) | (d & 2) << 1 | (d & 4) >> 1
    other = pen
    for bit in (1 << b for b in range(n_pen.bit_length() - 1)):
        flip = (1 - core) * int(d & bit > 0) + core * int(swapped & bit > 0)
        other = other + flip * bit * (1 - 2 * lax.rem(pen // bit, 2))
    return other


def kernel(n_pen, n_blk, rates, partner, side, orient, offset, state, inv_x, inv_y, out,
           planes, swept, op_x, op_xt, op_y, perm, layers,
           in_send, in_recv, out_send, out_recv, g_send, g_recv, own_sem, op_sem):
    blk = lax.axis_index("blk")
    pen = lax.axis_index("pen")
    rows = state.shape[3]
    z_per = planes.shape[1]
    gy, gx = planes.shape[2], planes.shape[3]

    order = (2, 4, 6, 3, 5, 7, 1) if n_pen == 8 else range(1, n_pen)
    partners = [partner_of(pen, d, n_pen) for d in order]

    barrier = pltpu.get_barrier_semaphore()
    for to in partners:
        pl.semaphore_signal(barrier, inc=1, device_id=(blk, to),
                            device_id_type=pl.DeviceIdType.MESH)
    for d in range(1, n_blk):
        pl.semaphore_signal(barrier, inc=1, device_id=(lax.rem(blk + d, n_blk), pen),
                            device_id_type=pl.DeviceIdType.MESH)
    pl.semaphore_wait(barrier, n_pen + n_blk - 2)

    def in_copy(z, to):
        return pltpu.make_async_remote_copy(
            src_ref=state.at[0, :, to * z_per + z],
            dst_ref=planes.at[:, z, pl.ds(pen * rows, rows)],
            send_sem=in_send.at[z, to], recv_sem=in_recv.at[z, pen],
            device_id=(blk, to), device_id_type=pl.DeviceIdType.MESH)

    def in_arrival(z, came):
        return pltpu.make_async_remote_copy(
            src_ref=state.at[0, :, came * z_per + z],
            dst_ref=planes.at[:, z, pl.ds(came * rows, rows)],
            send_sem=in_send.at[z, came], recv_sem=in_recv.at[z, came],
            device_id=(blk, came), device_id_type=pl.DeviceIdType.MESH)

    def in_own(z):
        return pltpu.make_async_copy(
            state.at[0, :, pen * z_per + z], planes.at[:, z, pl.ds(pen * rows, rows)], own_sem.at[0, z])

    def out_copy(z, to):
        return pltpu.make_async_remote_copy(
            src_ref=planes.at[:, z, pl.ds(to * rows, rows)],
            dst_ref=out.at[0, :, pen * z_per + z],
            send_sem=out_send.at[z, to], recv_sem=out_recv.at[z, pen],
            device_id=(blk, to), device_id_type=pl.DeviceIdType.MESH)

    def out_arrival(z, came):
        return pltpu.make_async_remote_copy(
            src_ref=planes.at[:, z, pl.ds(came * rows, rows)],
            dst_ref=out.at[0, :, came * z_per + z],
            send_sem=out_send.at[z, came], recv_sem=out_recv.at[z, came],
            device_id=(blk, came), device_id_type=pl.DeviceIdType.MESH)

    def out_own(z):
        return pltpu.make_async_copy(
            planes.at[:, z, pl.ds(pen * rows, rows)], out.at[0, :, pen * z_per + z], own_sem.at[1, z])

    def ghost_copy(slot, d):
        return pltpu.make_async_remote_copy(
            src_ref=layers.at[slot, blk], dst_ref=layers.at[slot, blk],
            send_sem=g_send.at[slot, d], recv_sem=g_recv.at[slot, d],
            device_id=(lax.rem(blk + d, n_blk), pen), device_id_type=pl.DeviceIdType.MESH)

    def ghost_arrival(slot, d):
        came = lax.rem(blk + n_blk - d, n_blk)
        return pltpu.make_async_remote_copy(
            src_ref=layers.at[slot, came], dst_ref=layers.at[slot, came],
            send_sem=g_send.at[slot, d], recv_sem=g_recv.at[slot, d],
            device_id=(came, pen), device_id_type=pl.DeviceIdType.MESH)

    def send_in(z):
        for to in partners:
            in_copy(z, to).start()
        in_own(z).start()

    ahead = min(2, z_per)
    pl.loop(0, ahead)(send_in)

    load_x = pltpu.make_async_copy(inv_x.at[0], op_x, op_sem.at[0])
    load_y = pltpu.make_async_copy(inv_y.at[0], op_y, op_sem.at[1])
    load_x.start()
    load_y.start()

    at_j = lax.broadcasted_iota(jnp.int32, (gy, gy), 0)
    at_y = lax.broadcasted_iota(jnp.int32, (gy, gy), 1)
    for k in range(2):
        take = jnp.where(orient[0, k] == 1, gy - 1 - at_j, at_j) + offset[0, k] * rows
        take = jnp.where(take >= gy, take - gy, take)
        perm[k] = jnp.where(take == at_y, 1.0, 0.0).astype(jnp.bfloat16)
    eye = jnp.where(at_j == at_y, 1.0, 0.0).astype(jnp.bfloat16)
    load_x.wait()
    for f in range(2):
        op_xt[f] = dot_nt(eye, op_x[f]).astype(jnp.bfloat16)
    load_y.wait()

    pick_row = lax.broadcasted_iota(jnp.int32, (16, LANES), 0)
    pick_lane = lax.broadcasted_iota(jnp.int32, (16, LANES), 1)
    lane = lax.broadcasted_iota(jnp.int32, (gy, LANES), 1)
    ends = ((0, 0), (gx - LANES, LANES - 1))
    half = gx // 2

    def send_layers(z, slot):
        mine = jnp.zeros((16, gy), jnp.float32)
        for k, (first, at) in enumerate(ends):
            for f in range(2):
                pick = jnp.where((pick_row == 2 * k + f) & (pick_lane == at), 1.0, 0.0).astype(jnp.bfloat16)
                mine += dot_nt(pick, planes[f, z, :, first:first + LANES])
        layers[slot, blk] = mine.astype(jnp.bfloat16)
        for d in range(1, n_blk):
            ghost_copy(slot, d).start()

    def sweep(z, slot):
        for d in range(1, n_blk):
            ghost_arrival(slot, d).wait_recv()
        for k, (first, at) in enumerate(ends):
            layer = layers[slot, 0]
            for b in range(1, n_blk):
                layer = jnp.where(partner[0, k] == b, layers[slot, b], layer)
            ghosts = dot_nt(perm[k], layer)
            for f in range(2):
                ghost = jnp.where(side[0, k] == 1, ghosts[:, 2 + f:3 + f], ghosts[:, f:f + 1])
                cells = planes[f, z, :, first:first + LANES].astype(jnp.float32)
                planes[f, z, :, first:first + LANES] = (
                    cells + jnp.where(lane == at, ghost, 0.0)).astype(jnp.bfloat16)

        for f in range(2):
            for n in range(2):
                swept[f, :, n * half:(n + 1) * half] = dot(
                    planes[f, z], op_xt[f, :, n * half:(n + 1) * half]).astype(jnp.bfloat16)
        for n in range(2):
            proton = dot(op_y[0], swept[0, :, n * half:(n + 1) * half])
            carbon = dot(op_y[1], swept[1, :, n * half:(n + 1) * half])
            new_proton = proton - (rates[0, 0] * proton + rates[0, 2] * carbon)
            new_carbon = carbon - (rates[0, 1] * carbon + rates[0, 2] * proton)
            planes[0, z, :, n * half:(n + 1) * half] = new_proton.astype(jnp.bfloat16)
            planes[1, z, :, n * half:(n + 1) * half] = new_carbon.astype(jnp.bfloat16)

    @pl.loop(0, z_per + 1)
    def _(z):
        @pl.when(z < z_per)
        def _():
            for came in partners:
                in_arrival(z, came).wait_recv()
            in_own(z).wait()
            pl.when(z + ahead < z_per)(lambda: send_in(z + ahead))
            send_layers(z, STEPS * z)

        @pl.when(z > 0)
        def _():
            sweep(z - 1, STEPS * z - 1)
            for to in partners:
                out_copy(z - 1, to).start()
            out_own(z - 1).start()

        @pl.when(z < z_per)
        def _():
            sweep(z, STEPS * z)
            send_layers(z, STEPS * z + 1)

    @pl.loop(0, z_per)
    def _(z):
        for to in partners:
            in_copy(z, to).wait_send()
            out_copy(z, to).wait_send()
            out_arrival(z, to).wait_recv()
        out_own(z).wait()
        for step in range(STEPS):
            for d in range(1, n_blk):
                ghost_copy(z * STEPS + step, d).wait_send()


def solution(mesh):
    n_pen, n_blk = mesh.shape["pen"], mesh.shape["blk"]

    def local(state, inverse_x, inverse_y, rates, partner, face_side, orient, offset):
        _, fields, gz, rows, gx = state.shape
        z_per, gy = gz // n_pen, rows * n_pen
        slots = z_per * STEPS
        keep = functools.partial(pltpu.with_memory_space_constraint, memory_space=pltpu.HBM)
        smem = pl.BlockSpec(memory_space=pltpu.SMEM)
        anywhere = pl.BlockSpec(memory_space=pl.ANY)
        bf16 = jnp.bfloat16
        return pl.pallas_call(
            functools.partial(kernel, n_pen, n_blk),
            out_shape=pltpu.VMEM(state.shape, state.dtype),
            in_specs=[smem] * 5 + [anywhere] * 3,
            out_specs=anywhere,
            scratch_shapes=[
                pltpu.VMEM((fields, z_per, gy, gx), bf16),
                pltpu.VMEM((fields, gy, gx), bf16),
                pltpu.VMEM((fields, gx, gx), bf16),
                pltpu.VMEM((fields, gx, gx), bf16),
                pltpu.VMEM((fields, gy, gy), bf16),
                pltpu.VMEM((2, gy, gy), bf16),
                pltpu.VMEM((slots, n_blk, 16, gy), bf16),
                pltpu.SemaphoreType.DMA((z_per, n_pen)),
                pltpu.SemaphoreType.DMA((z_per, n_pen)),
                pltpu.SemaphoreType.DMA((z_per, n_pen)),
                pltpu.SemaphoreType.DMA((z_per, n_pen)),
                pltpu.SemaphoreType.DMA((slots, n_blk)),
                pltpu.SemaphoreType.DMA((slots, n_blk)),
                pltpu.SemaphoreType.DMA((2, z_per)),
                pltpu.SemaphoreType.DMA((2,)),
            ],
            compiler_params=pltpu.CompilerParams(
                collective_id=0, has_side_effects=True, vmem_limit_bytes=48 * 1024 * 1024),
            cost_estimate=pl.CostEstimate(
                flops=8 * STEPS * z_per * gy * gx * (gx + gy) // 2,
                bytes_accessed=4 * state.size + 8 * gx * gx, transcendentals=0),
        )(*map(keep, (rates, partner, face_side, orient, offset, state, inverse_x, inverse_y)))

    line = P("blk", None)
    return jax.shard_map(
        local,
        mesh=mesh,
        in_specs=(
            P("blk", None, None, "pen", None),
            P("blk", None, None, None),
            P("blk", None, None, None),
            line, line, line, line, line,
        ),
        out_specs=P("blk", None, None, "pen", None),
        check_vma=False,
    )
```

```python
import functools
import jax
import jax.numpy as jnp
from jax import lax
from jax.experimental import pallas as pl
from jax.experimental.pallas import tpu as pltpu
from jax.sharding import PartitionSpec as P

STEPS = 2
LANES = 128
NT = (((1,), (1,)), ((), ()))


def dot(a, b):
    return jnp.dot(a, b, preferred_element_type=jnp.float32)


def dot_nt(a, b):
    return lax.dot_general(a, b, NT, preferred_element_type=jnp.float32)


def partner_of(pen, d, n_pen):
    if n_pen & (n_pen - 1) or n_pen < 8:
        return lax.rem(pen + d, n_pen)
    core = lax.rem(pen, 2)
    swapped = (d & ~6) | (d & 2) << 1 | (d & 4) >> 1
    other = pen
    for bit in (1 << b for b in range(n_pen.bit_length() - 1)):
        flip = (1 - core) * int(d & bit > 0) + core * int(swapped & bit > 0)
        other = other + flip * bit * (1 - 2 * lax.rem(pen // bit, 2))
    return other


def kernel(n_pen, n_blk, rates, partner, side, orient, offset, state, inv_x, inv_y, out,
           planes, swept, op_x, op_xt, op_y, perm, layers,
           in_send, in_recv, out_send, out_recv, g_send, g_recv, own_sem, op_sem):
    blk = lax.axis_index("blk")
    pen = lax.axis_index("pen")
    rows = state.shape[3]
    z_per = planes.shape[1]
    gy, gx = planes.shape[2], planes.shape[3]

    order = (2, 4, 6, 3, 5, 7, 1) if n_pen == 8 else range(1, n_pen)
    partners = [partner_of(pen, d, n_pen) for d in order]

    barrier = pltpu.get_barrier_semaphore()
    for to in partners:
        pl.semaphore_signal(barrier, inc=1, device_id=(blk, to),
                            device_id_type=pl.DeviceIdType.MESH)
    for d in range(1, n_blk):
        pl.semaphore_signal(barrier, inc=1, device_id=(lax.rem(blk + d, n_blk), pen),
                            device_id_type=pl.DeviceIdType.MESH)
    pl.semaphore_wait(barrier, n_pen + n_blk - 2)

    def in_copy(z, to):
        return pltpu.make_async_remote_copy(
            src_ref=state.at[0, :, to * z_per + z],
            dst_ref=planes.at[:, z, pl.ds(pen * rows, rows)],
            send_sem=in_send.at[z, to], recv_sem=in_recv.at[z, pen],
            device_id=(blk, to), device_id_type=pl.DeviceIdType.MESH)

    def in_arrival(z, came):
        return pltpu.make_async_remote_copy(
            src_ref=state.at[0, :, came * z_per + z],
            dst_ref=planes.at[:, z, pl.ds(came * rows, rows)],
            send_sem=in_send.at[z, came], recv_sem=in_recv.at[z, came],
            device_id=(blk, came), device_id_type=pl.DeviceIdType.MESH)

    def in_own(z):
        return pltpu.make_async_copy(
            state.at[0, :, pen * z_per + z], planes.at[:, z, pl.ds(pen * rows, rows)], own_sem.at[0, z])

    def out_copy(z, to):
        return pltpu.make_async_remote_copy(
            src_ref=planes.at[:, z, pl.ds(to * rows, rows)],
            dst_ref=out.at[0, :, pen * z_per + z],
            send_sem=out_send.at[z, to], recv_sem=out_recv.at[z, pen],
            device_id=(blk, to), device_id_type=pl.DeviceIdType.MESH)

    def out_arrival(z, came):
        return pltpu.make_async_remote_copy(
            src_ref=planes.at[:, z, pl.ds(came * rows, rows)],
            dst_ref=out.at[0, :, came * z_per + z],
            send_sem=out_send.at[z, came], recv_sem=out_recv.at[z, came],
            device_id=(blk, came), device_id_type=pl.DeviceIdType.MESH)

    def out_own(z):
        return pltpu.make_async_copy(
            planes.at[:, z, pl.ds(pen * rows, rows)], out.at[0, :, pen * z_per + z], own_sem.at[1, z])

    def ghost_copy(slot, d):
        return pltpu.make_async_remote_copy(
            src_ref=layers.at[slot, blk], dst_ref=layers.at[slot, blk],
            send_sem=g_send.at[slot, d], recv_sem=g_recv.at[slot, d],
            device_id=(lax.rem(blk + d, n_blk), pen), device_id_type=pl.DeviceIdType.MESH)

    def ghost_arrival(slot, d):
        came = lax.rem(blk + n_blk - d, n_blk)
        return pltpu.make_async_remote_copy(
            src_ref=layers.at[slot, came], dst_ref=layers.at[slot, came],
            send_sem=g_send.at[slot, d], recv_sem=g_recv.at[slot, d],
            device_id=(came, pen), device_id_type=pl.DeviceIdType.MESH)

    def send_in(z):
        for to in partners:
            in_copy(z, to).start()
        in_own(z).start()

    pl.loop(0, z_per)(send_in)

    load_x = pltpu.make_async_copy(inv_x.at[0], op_x, op_sem.at[0])
    load_y = pltpu.make_async_copy(inv_y.at[0], op_y, op_sem.at[1])
    load_x.start()
    load_y.start()

    at_j = lax.broadcasted_iota(jnp.int32, (gy, gy), 0)
    at_y = lax.broadcasted_iota(jnp.int32, (gy, gy), 1)
    for k in range(2):
        take = jnp.where(orient[0, k] == 1, gy - 1 - at_j, at_j) + offset[0, k] * rows
        take = jnp.where(take >= gy, take - gy, take)
        perm[k] = jnp.where(take == at_y, 1.0, 0.0).astype(jnp.bfloat16)
    eye = jnp.where(at_j == at_y, 1.0, 0.0).astype(jnp.bfloat16)
    load_x.wait()
    for f in range(2):
        op_xt[f] = dot_nt(eye, op_x[f]).astype(jnp.bfloat16)
    load_y.wait()

    pick_row = lax.broadcasted_iota(jnp.int32, (16, LANES), 0)
    pick_lane = lax.broadcasted_iota(jnp.int32, (16, LANES), 1)
    lane = lax.broadcasted_iota(jnp.int32, (gy, LANES), 1)
    ends = ((0, 0), (gx - LANES, LANES - 1))
    half = gx // 2

    def send_layers(z, slot):
        mine = jnp.zeros((16, gy), jnp.float32)
        for k, (first, at) in enumerate(ends):
            for f in range(2):
                pick = jnp.where((pick_row == 2 * k + f) & (pick_lane == at), 1.0, 0.0).astype(jnp.bfloat16)
                mine += dot_nt(pick, planes[f, z, :, first:first + LANES])
        layers[slot, blk] = mine.astype(jnp.bfloat16)
        for d in range(1, n_blk):
            ghost_copy(slot, d).start()

    def sweep(z, slot):
        for d in range(1, n_blk):
            ghost_arrival(slot, d).wait_recv()
        for k, (first, at) in enumerate(ends):
            layer = layers[slot, 0]
            for b in range(1, n_blk):
                layer = jnp.where(partner[0, k] == b, layers[slot, b], layer)
            ghosts = dot_nt(perm[k], layer)
            for f in range(2):
                ghost = jnp.where(side[0, k] == 1, ghosts[:, 2 + f:3 + f], ghosts[:, f:f + 1])
                cells = planes[f, z, :, first:first + LANES].astype(jnp.float32)
                planes[f, z, :, first:first + LANES] = (
                    cells + jnp.where(lane == at, ghost, 0.0)).astype(jnp.bfloat16)

        for f in range(2):
            for n in range(2):
                swept[f, :, n * half:(n + 1) * half] = dot(
                    planes[f, z], op_xt[f, :, n * half:(n + 1) * half]).astype(jnp.bfloat16)
        for n in range(2):
            proton = dot(op_y[0], swept[0, :, n * half:(n + 1) * half])
            carbon = dot(op_y[1], swept[1, :, n * half:(n + 1) * half])
            new_proton = proton - (rates[0, 0] * proton + rates[0, 2] * carbon)
            new_carbon = carbon - (rates[0, 1] * carbon + rates[0, 2] * proton)
            planes[0, z, :, n * half:(n + 1) * half] = new_proton.astype(jnp.bfloat16)
            planes[1, z, :, n * half:(n + 1) * half] = new_carbon.astype(jnp.bfloat16)

    @pl.loop(0, z_per + 1)
    def _(z):
        @pl.when(z < z_per)
        def _():
            for came in partners:
                in_arrival(z, came).wait_recv()
            in_own(z).wait()
            send_layers(z, STEPS * z)

        @pl.when(z > 0)
        def _():
            sweep(z - 1, STEPS * z - 1)
            for to in partners:
                out_copy(z - 1, to).start()
            out_own(z - 1).start()

        @pl.when(z < z_per)
        def _():
            sweep(z, STEPS * z)
            send_layers(z, STEPS * z + 1)

    @pl.loop(0, z_per)
    def _(z):
        for to in partners:
            in_copy(z, to).wait_send()
            out_copy(z, to).wait_send()
            out_arrival(z, to).wait_recv()
        out_own(z).wait()
        for step in range(STEPS):
            for d in range(1, n_blk):
                ghost_copy(z * STEPS + step, d).wait_send()


def solution(mesh):
    n_pen, n_blk = mesh.shape["pen"], mesh.shape["blk"]

    def local(state, inverse_x, inverse_y, rates, partner, face_side, orient, offset):
        _, fields, gz, rows, gx = state.shape
        z_per, gy = gz // n_pen, rows * n_pen
        slots = z_per * STEPS
        keep = functools.partial(pltpu.with_memory_space_constraint, memory_space=pltpu.HBM)
        smem = pl.BlockSpec(memory_space=pltpu.SMEM)
        anywhere = pl.BlockSpec(memory_space=pl.ANY)
        bf16 = jnp.bfloat16
        return pl.pallas_call(
            functools.partial(kernel, n_pen, n_blk),
            out_shape=pltpu.VMEM(state.shape, state.dtype),
            in_specs=[smem] * 5 + [anywhere] * 3,
            out_specs=anywhere,
            scratch_shapes=[
                pltpu.VMEM((fields, z_per, gy, gx), bf16),
                pltpu.VMEM((fields, gy, gx), bf16),
                pltpu.VMEM((fields, gx, gx), bf16),
                pltpu.VMEM((fields, gx, gx), bf16),
                pltpu.VMEM((fields, gy, gy), bf16),
                pltpu.VMEM((2, gy, gy), bf16),
                pltpu.VMEM((slots, n_blk, 16, gy), bf16),
                pltpu.SemaphoreType.DMA((z_per, n_pen)),
                pltpu.SemaphoreType.DMA((z_per, n_pen)),
                pltpu.SemaphoreType.DMA((z_per, n_pen)),
                pltpu.SemaphoreType.DMA((z_per, n_pen)),
                pltpu.SemaphoreType.DMA((slots, n_blk)),
                pltpu.SemaphoreType.DMA((slots, n_blk)),
                pltpu.SemaphoreType.DMA((2, z_per)),
                pltpu.SemaphoreType.DMA((2,)),
            ],
            compiler_params=pltpu.CompilerParams(
                collective_id=0, has_side_effects=True, vmem_limit_bytes=48 * 1024 * 1024),
            cost_estimate=pl.CostEstimate(
                flops=8 * STEPS * z_per * gy * gx * (gx + gy) // 2,
                bytes_accessed=4 * state.size + 8 * gx * gx, transcendentals=0),
        )(*map(keep, (rates, partner, face_side, orient, offset, state, inverse_x, inverse_y)))

    line = P("blk", None)
    return jax.shard_map(
        local,
        mesh=mesh,
        in_specs=(
            P("blk", None, None, "pen", None),
            P("blk", None, None, None),
            P("blk", None, None, None),
            line, line, line, line, line,
        ),
        out_specs=P("blk", None, None, "pen", None),
        check_vma=False,
    )
```

```python
import functools
import jax
import jax.numpy as jnp
from jax import lax
from jax.experimental import pallas as pl
from jax.experimental.pallas import tpu as pltpu
from jax.sharding import PartitionSpec as P

STEPS = 2
LANES = 128
NT = (((1,), (1,)), ((), ()))


def dot(a, b):
    return jnp.dot(a, b, preferred_element_type=jnp.float32)


def dot_nt(a, b):
    return lax.dot_general(a, b, NT, preferred_element_type=jnp.float32)


def kernel(n_pen, n_blk, rates, partner, side, orient, offset, state, inv_x, inv_y, out,
           planes, swept, op_x, op_xt, op_y, perm, layers,
           in_send, in_recv, out_send, out_recv, g_send, g_recv, own_sem, op_sem):
    blk = lax.axis_index("blk")
    pen = lax.axis_index("pen")
    rows = state.shape[3]
    z_per = planes.shape[1]
    gy, gx = planes.shape[2], planes.shape[3]

    partners = [lax.rem(pen + d, n_pen) for d in range(1, n_pen)]

    barrier = pltpu.get_barrier_semaphore()
    for to in partners:
        pl.semaphore_signal(barrier, inc=1, device_id=(blk, to),
                            device_id_type=pl.DeviceIdType.MESH)
    for d in range(1, n_blk):
        pl.semaphore_signal(barrier, inc=1, device_id=(lax.rem(blk + d, n_blk), pen),
                            device_id_type=pl.DeviceIdType.MESH)
    pl.semaphore_wait(barrier, n_pen + n_blk - 2)

    def in_copy(z, to):
        return pltpu.make_async_remote_copy(
            src_ref=state.at[0, :, to * z_per + z],
            dst_ref=planes.at[:, z, pl.ds(pen * rows, rows)],
            send_sem=in_send.at[z, to], recv_sem=in_recv.at[z, pen],
            device_id=(blk, to), device_id_type=pl.DeviceIdType.MESH)

    def in_arrival(z, came):
        return pltpu.make_async_remote_copy(
            src_ref=state.at[0, :, came * z_per + z],
            dst_ref=planes.at[:, z, pl.ds(came * rows, rows)],
            send_sem=in_send.at[z, came], recv_sem=in_recv.at[z, came],
            device_id=(blk, came), device_id_type=pl.DeviceIdType.MESH)

    def in_own(z):
        return pltpu.make_async_copy(
            state.at[0, :, pen * z_per + z], planes.at[:, z, pl.ds(pen * rows, rows)], own_sem.at[0, z])

    def out_copy(z, to):
        return pltpu.make_async_remote_copy(
            src_ref=planes.at[:, z, pl.ds(to * rows, rows)],
            dst_ref=out.at[0, :, pen * z_per + z],
            send_sem=out_send.at[z, to], recv_sem=out_recv.at[z, pen],
            device_id=(blk, to), device_id_type=pl.DeviceIdType.MESH)

    def out_arrival(z, came):
        return pltpu.make_async_remote_copy(
            src_ref=planes.at[:, z, pl.ds(came * rows, rows)],
            dst_ref=out.at[0, :, came * z_per + z],
            send_sem=out_send.at[z, came], recv_sem=out_recv.at[z, came],
            device_id=(blk, came), device_id_type=pl.DeviceIdType.MESH)

    def out_own(z):
        return pltpu.make_async_copy(
            planes.at[:, z, pl.ds(pen * rows, rows)], out.at[0, :, pen * z_per + z], own_sem.at[1, z])

    def ghost_copy(slot, d):
        return pltpu.make_async_remote_copy(
            src_ref=layers.at[slot, blk], dst_ref=layers.at[slot, blk],
            send_sem=g_send.at[slot, d], recv_sem=g_recv.at[slot, d],
            device_id=(lax.rem(blk + d, n_blk), pen), device_id_type=pl.DeviceIdType.MESH)

    def ghost_arrival(slot, d):
        came = lax.rem(blk + n_blk - d, n_blk)
        return pltpu.make_async_remote_copy(
            src_ref=layers.at[slot, came], dst_ref=layers.at[slot, came],
            send_sem=g_send.at[slot, d], recv_sem=g_recv.at[slot, d],
            device_id=(came, pen), device_id_type=pl.DeviceIdType.MESH)

    def send_in(z):
        for to in partners:
            in_copy(z, to).start()
        in_own(z).start()

    pl.loop(0, z_per)(send_in)

    load_x = pltpu.make_async_copy(inv_x.at[0], op_x, op_sem.at[0])
    load_y = pltpu.make_async_copy(inv_y.at[0], op_y, op_sem.at[1])
    load_x.start()
    load_y.start()

    at_j = lax.broadcasted_iota(jnp.int32, (gy, gy), 0)
    at_y = lax.broadcasted_iota(jnp.int32, (gy, gy), 1)
    for k in range(2):
        take = jnp.where(orient[0, k] == 1, gy - 1 - at_j, at_j) + offset[0, k] * rows
        take = jnp.where(take >= gy, take - gy, take)
        perm[k] = jnp.where(take == at_y, 1.0, 0.0).astype(jnp.bfloat16)
    eye = jnp.where(at_j == at_y, 1.0, 0.0).astype(jnp.bfloat16)
    load_x.wait()
    for f in range(2):
        op_xt[f] = dot_nt(eye, op_x[f]).astype(jnp.bfloat16)
    load_y.wait()

    pick_row = lax.broadcasted_iota(jnp.int32, (16, LANES), 0)
    pick_lane = lax.broadcasted_iota(jnp.int32, (16, LANES), 1)
    lane = lax.broadcasted_iota(jnp.int32, (gy, LANES), 1)
    ends = ((0, 0), (gx - LANES, LANES - 1))
    half = gx // 2

    def send_layers(z, slot):
        mine = jnp.zeros((16, gy), jnp.float32)
        for k, (first, at) in enumerate(ends):
            for f in range(2):
                pick = jnp.where((pick_row == 2 * k + f) & (pick_lane == at), 1.0, 0.0).astype(jnp.bfloat16)
                mine += dot_nt(pick, planes[f, z, :, first:first + LANES])
        layers[slot, blk] = mine.astype(jnp.bfloat16)
        for d in range(1, n_blk):
            ghost_copy(slot, d).start()

    def sweep(z, slot):
        for d in range(1, n_blk):
            ghost_arrival(slot, d).wait_recv()
        for k, (first, at) in enumerate(ends):
            layer = layers[slot, 0]
            for b in range(1, n_blk):
                layer = jnp.where(partner[0, k] == b, layers[slot, b], layer)
            ghosts = dot_nt(perm[k], layer)
            for f in range(2):
                ghost = jnp.where(side[0, k] == 1, ghosts[:, 2 + f:3 + f], ghosts[:, f:f + 1])
                cells = planes[f, z, :, first:first + LANES].astype(jnp.float32)
                planes[f, z, :, first:first + LANES] = (
                    cells + jnp.where(lane == at, ghost, 0.0)).astype(jnp.bfloat16)

        for f in range(2):
            for n in range(2):
                swept[f, :, n * half:(n + 1) * half] = dot(
                    planes[f, z], op_xt[f, :, n * half:(n + 1) * half]).astype(jnp.bfloat16)
        for n in range(2):
            proton = dot(op_y[0], swept[0, :, n * half:(n + 1) * half])
            carbon = dot(op_y[1], swept[1, :, n * half:(n + 1) * half])
            new_proton = proton - (rates[0, 0] * proton + rates[0, 2] * carbon)
            new_carbon = carbon - (rates[0, 1] * carbon + rates[0, 2] * proton)
            planes[0, z, :, n * half:(n + 1) * half] = new_proton.astype(jnp.bfloat16)
            planes[1, z, :, n * half:(n + 1) * half] = new_carbon.astype(jnp.bfloat16)

    @pl.loop(0, z_per + 1)
    def _(z):
        @pl.when(z < z_per)
        def _():
            for came in partners:
                in_arrival(z, came).wait_recv()
            in_own(z).wait()
            send_layers(z, STEPS * z)

        @pl.when(z > 0)
        def _():
            sweep(z - 1, STEPS * z - 1)
            for to in partners:
                out_copy(z - 1, to).start()
            out_own(z - 1).start()

        @pl.when(z < z_per)
        def _():
            sweep(z, STEPS * z)
            send_layers(z, STEPS * z + 1)

    @pl.loop(0, z_per)
    def _(z):
        for to in partners:
            in_copy(z, to).wait_send()
            out_copy(z, to).wait_send()
            out_arrival(z, to).wait_recv()
        out_own(z).wait()
        for step in range(STEPS):
            for d in range(1, n_blk):
                ghost_copy(z * STEPS + step, d).wait_send()


def solution(mesh):
    n_pen, n_blk = mesh.shape["pen"], mesh.shape["blk"]

    def local(state, inverse_x, inverse_y, rates, partner, face_side, orient, offset):
        _, fields, gz, rows, gx = state.shape
        z_per, gy = gz // n_pen, rows * n_pen
        slots = z_per * STEPS
        keep = functools.partial(pltpu.with_memory_space_constraint, memory_space=pltpu.HBM)
        smem = pl.BlockSpec(memory_space=pltpu.SMEM)
        anywhere = pl.BlockSpec(memory_space=pl.ANY)
        bf16 = jnp.bfloat16
        return pl.pallas_call(
            functools.partial(kernel, n_pen, n_blk),
            out_shape=pltpu.VMEM(state.shape, state.dtype),
            in_specs=[smem] * 5 + [anywhere] * 3,
            out_specs=anywhere,
            scratch_shapes=[
                pltpu.VMEM((fields, z_per, gy, gx), bf16),
                pltpu.VMEM((fields, gy, gx), bf16),
                pltpu.VMEM((fields, gx, gx), bf16),
                pltpu.VMEM((fields, gx, gx), bf16),
                pltpu.VMEM((fields, gy, gy), bf16),
                pltpu.VMEM((2, gy, gy), bf16),
                pltpu.VMEM((slots, n_blk, 16, gy), bf16),
                pltpu.SemaphoreType.DMA((z_per, n_pen)),
                pltpu.SemaphoreType.DMA((z_per, n_pen)),
                pltpu.SemaphoreType.DMA((z_per, n_pen)),
                pltpu.SemaphoreType.DMA((z_per, n_pen)),
                pltpu.SemaphoreType.DMA((slots, n_blk)),
                pltpu.SemaphoreType.DMA((slots, n_blk)),
                pltpu.SemaphoreType.DMA((2, z_per)),
                pltpu.SemaphoreType.DMA((2,)),
            ],
            compiler_params=pltpu.CompilerParams(
                collective_id=0, has_side_effects=True, vmem_limit_bytes=48 * 1024 * 1024),
            cost_estimate=pl.CostEstimate(
                flops=8 * STEPS * z_per * gy * gx * (gx + gy) // 2,
                bytes_accessed=4 * state.size + 8 * gx * gx, transcendentals=0),
        )(*map(keep, (rates, partner, face_side, orient, offset, state, inverse_x, inverse_y)))

    line = P("blk", None)
    return jax.shard_map(
        local,
        mesh=mesh,
        in_specs=(
            P("blk", None, None, "pen", None),
            P("blk", None, None, None),
            P("blk", None, None, None),
            line, line, line, line, line,
        ),
        out_specs=P("blk", None, None, "pen", None),
        check_vma=False,
    )
```
